256 devices in a mesh: ka: 128 (over z, y, x), ga: 2 (over core).
Axes of the slice: x: 4, y: 4, z: 8, core: 2. Of those that a mesh axis runs over, the one named last changes fastest.
Arguments:
- pair_dens: bfloat16 [4096, 40, 1792], P('ka', None, 'ga'), may hold values from -6 to 6
- counts: int32 [4096], P('ka'), may hold values from 2 to 40, as said below
- q_index: int32 [4096, 2], P('ka'), may hold values from 0 to 1, each once within a row
- w_tiles: bfloat16 [2, 1792, 1792], P(None, 'ga', 'ka'), as said below
- partner: bfloat16 [4096, 2, 40, 1792], P('ka', None, None, 'ga'), may hold values from -0.125 to 0.125
Outputs:
- kernel: float32 [4096, 2, 1600], P('ka')
The draws below stay inside these ranges and needn't reach their ends.
Inputs may be any that keep to these rules, and one draw needn't show every extreme that they name: `counts`: some k point has 40 pairs; the pairs of the 32 k points of one index of ka sum to at most 960, and some index reaches it; the pairs of indices i and i + 64 together sum to at most 1280, and some such two reach it. Each tile is symmetric: w_tiles[b, g, h] = w_tiles[b, h, g].
All inputs are finite; a program needn't handle non-finite values.
Results may differ from the reference program's by a relative error of at most 0.0029.
Values may be sent and summed in bfloat16 or wider, within the bound.
A program may use at most 128 MiB of HBM per device.

```python
import jax
import jax.numpy as jnp
from jax import lax

NG = 1792
PMAX = 40
PC = 40
NQB = 2
K_DEV = 32
NK = 4096
N_KA = 128


def draw_counts(key, part):
    key = jax.random.fold_in(key, 11)
    key_level, key_base, key_order, key_busy = jax.random.split(key, 4)
    level = jax.random.randint(key_level, (N_KA, 1), 1, 3)
    base_draw = jax.random.randint(key_base, (N_KA, K_DEV), 0, PMAX - 1)
    pair_counts = 2 + base_draw * level // 8
    order = jax.random.permutation(key_order, K_DEV)
    busiest_counts = jnp.where(order < K_DEV // 2, PMAX, PMAX // 2)
    busiest = jax.random.randint(key_busy, (), 0, N_KA)
    helper = (busiest + N_KA // 2) % N_KA
    rows = jnp.arange(N_KA)[:, None]
    pair_counts = jnp.where(rows == helper, PMAX // 4, pair_counts)
    pair_counts = jnp.where(rows == busiest, busiest_counts[None, :], pair_counts)
    return pair_counts.reshape(-1).astype(jnp.int32)


def draw_w_tiles(key, part):
    key = jax.random.fold_in(key, 23)
    raw_draw = jax.random.normal(key, (NQB, NG, NG), jnp.float32)
    symmetric = (raw_draw + jnp.swapaxes(raw_draw, 1, 2)) * 0.5 ** 0.5
    return (symmetric * NG ** (-0.5)).astype(jnp.bfloat16)


def level_of(own_key, shape, shards, least, top_value):
    def one(position, blocks):
        heights = jax.random.uniform(jax.random.fold_in(jax.random.fold_in(own_key, 6), position), (blocks,), jnp.float32, least / len(shards), top_value / len(shards))
        return jnp.repeat(jnp.exp(heights), shape[position] // blocks).reshape((-1,) + (1,) * (len(shape) - position - 1))

    loudness = one(*shards[0])
    for cut in shards[1:]:
        loudness = loudness * one(*cut)
    return loudness


def normal_values(stream_key, extent, deviation, most, cuts=(), kind=jnp.bfloat16):
    gain = level_of(stream_key, extent, cuts, -0.22, 0.18) if cuts else 1.0
    entries = jax.random.normal(stream_key, extent, jnp.float32) * deviation * gain
    return jnp.minimum(jnp.maximum(entries, -most), most).astype(kind)


def setup_inputs(seed: int = 0) -> dict:
    key_list = jax.random.split(jax.random.key(seed), 6)
    return {
        "pair_dens": normal_values(key_list[0], (NK, PMAX, NG), 1.0, 6.0, ((0, 128), (2, 2))),
        "counts": draw_counts(jax.random.fold_in(key_list[5], 71), 0),
        "q_index": jax.vmap(lambda own: jax.random.permutation(own, NQB))(jax.random.split(key_list[2], NK)).reshape((NK, NQB)).astype(jnp.int32),
        "w_tiles": draw_w_tiles(jax.random.fold_in(key_list[5], 71), 0),
        "partner": normal_values(key_list[4], (NK, NQB, PC, NG), NG ** -0.5, 0.125, ((0, 128), (3, 2))),
    }


def reference(pair_dens, counts, q_index, w_tiles, partner):
    dens_blocks = pair_dens.reshape(N_KA, K_DEV * PMAX, NG)
    count_blocks = counts.reshape(N_KA, K_DEV)
    index_blocks = q_index.reshape(N_KA, K_DEV, NQB)
    partner_blocks = partner.reshape(N_KA, K_DEV, NQB, PC, NG)

    def one_block(block_items):
        pair_rows, block_counts, block_index, block_partner = block_items
        screened = jnp.stack([jnp.dot(pair_rows, w_tiles[tile], preferred_element_type=jnp.float32).astype(jnp.bfloat16) for tile in range(NQB)])
        tile_grid = screened.reshape(NQB, K_DEV, PMAX, NG).astype(jnp.float32)
        per_tile = jnp.einsum("bkpg,kjcg->bkjpc", tile_grid, block_partner.astype(jnp.float32), precision=lax.Precision.HIGHEST)
        selector = block_index[None, :, :] == jnp.arange(NQB, dtype=jnp.int32)[:, None, None]
        chosen = jnp.sum(jnp.where(selector[:, :, :, None, None], per_tile, jnp.float32(0.0)), axis=0)
        live_mask = jnp.arange(PMAX, dtype=jnp.int32)[None, None, :, None] < block_counts[:, None, None, None]
        return jnp.where(live_mask, chosen, jnp.float32(0.0)).reshape(K_DEV, NQB, PMAX * PC)

    result = lax.map(one_block, (dens_blocks, count_blocks, index_blocks, partner_blocks))
    return result.reshape(NK, NQB, PMAX * PC)
```

```python
import jax
import jax.numpy as jnp
from jax import lax
from jax.experimental import pallas as pl
from jax.experimental.pallas import tpu as pltpu
from jax.sharding import PartitionSpec as P

MESH = pl.DeviceIdType.MESH
BF16, F32 = jnp.bfloat16, jnp.float32

NX, NY, NZ = 4, 4, 8
NODES = NX * NY * NZ
KP, SLOTS, PC = 32, 40, 40
ROWS = KP * SLOTS
NG, HALF = 1792, 896
BLK, MXU = 128, 256
OWN_ROWS = NG // NODES
TILE = 16
STRIPS = NG // TILE
ANTI = STRIPS // 2
SHIFT = 2 * NX * NY
ZSHIFT = SHIFT // (NX * NY)
MC = 256


def nt(a, b):
    return lax.dot_general(a, b, (((1,), (1,)), ((), ())), preferred_element_type=F32)


def nn(a, b):
    return jnp.dot(a, b, preferred_element_type=F32)


def kernel(pd, part, wt, cnt, qv, qs, out,
           pfull, qfull, praw, qsend, m1, m2, acc, rbuf, wraw, wplace, dbl, wn, kp, mine, other,
           s_loc, s_p0, r_p0, s_d2d, r_d2d, s_1, r_1, s_a2, r_a2, s_z, r_z, s_xy, r_xy):
    ka = lax.axis_index("ka")
    ga = lax.axis_index("ga")
    x, y, z = ka % NX, (ka // NX) % NY, ka // (NX * NY)

    def dev(dz=0, dy=0, dx=0):
        return (((z + dz + NZ) % NZ) * (NX * NY) + ((y + dy + NY) % NY) * NX + (x + dx + NX) % NX, ga)

    sibling = (ka, 1 - ga)
    strip = (ka + NODES - SHIFT) % NODES
    is_strip = strip < STRIPS
    is_anti = jnp.logical_and(strip >= STRIPS, strip < STRIPS + 8)

    bar = pltpu.get_barrier_semaphore()

    def greet(device):
        pl.semaphore_signal(bar, inc=1, device_id=device, device_id_type=MESH)

    t0 = (OWN_ROWS * ka) // TILE
    off = (OWN_ROWS * ka) % TILE
    crosses = off + OWN_ROWS > TILE
    n_waits = jnp.int32(9)
    for d in (1, 2, 3):
        greet(dev(dx=d))
        greet(dev(dy=d))
    greet(dev(dz=1))
    greet(dev(dz=-1))
    greet(sibling)

    first_src = (TILE * strip) // OWN_ROWS

    @pl.when(is_strip)
    def _():
        for a in range(2):
            for c in range(2):
                greet((first_src + a, c))

    @pl.when(is_anti)
    def _():
        for i in range(7):
            src = (TILE * (8 * i + strip - STRIPS)) // OWN_ROWS
            for a in range(2):
                greet((src + a, 1))

    one = ga == 1
    i32 = lambda b: jnp.where(b, jnp.int32(1), jnp.int32(0))
    n_waits = (n_waits + 2 + 2 * i32(crosses)
               + 2 * i32(jnp.logical_and(one, t0 < ANTI))
               + 2 * i32(jnp.logical_and(jnp.logical_and(one, crosses), t0 + 1 < ANTI)))

    own_cols = pl.ds(pl.multiple_of(ga * HALF, BLK), HALF)
    oth_cols = pl.ds(pl.multiple_of((1 - ga) * HALF, BLK), HALF)
    l_w = pltpu.make_async_copy(wt, wraw, s_loc.at[0])
    l_part = pltpu.make_async_copy(part, praw, s_loc.at[1])
    l_pd = pltpu.make_async_copy(pd, pfull.at[:, own_cols], s_loc.at[2])
    l_w.start()
    l_part.start()
    l_pd.start()

    l_w.wait()
    row = lax.broadcasted_iota(jnp.int32, (2 * TILE, TILE), 0)
    col = lax.broadcasted_iota(jnp.int32, (2 * TILE, TILE), 1)
    place = jnp.where(row == col + off, 1.0, 0.0).astype(BF16)
    for b in range(2):
        placed = nn(place, wraw[b]).astype(BF16)
        wplace[b, 0] = placed[:TILE]
        wplace[b, 1] = placed[TILE:]

    @pl.loop(0, ROWS // MC)
    def _(m):
        rows = pl.ds(m * MC, MC)
        for b in range(7):
            acc[b, rows, :] = jnp.zeros((MC, MXU), F32)

    l_part.wait()

    @pl.loop(0, KP // 2)
    def _(kk):
        keep, send = [], []
        for h in range(2):
            k = 2 * kk + h
            both = praw[pl.ds(80 * k, 80), :].astype(F32)
            zero_first = qs[2 * k] == ga
            keep.append(jnp.where(zero_first, both[:40], both[40:]))
            send.append(jnp.where(zero_first, both[40:], both[:40]))
        rows = pl.ds(80 * kk, 80)
        qfull[rows, own_cols] = jnp.concatenate(keep, axis=0).astype(BF16)
        qsend[rows, :] = jnp.concatenate(send, axis=0).astype(BF16)

    pl.semaphore_wait(bar, n_waits)

    p0 = []

    def push0(cond, src, dst, target, sem):
        copy = pltpu.make_async_remote_copy(src, dst, s_p0.at[sem], r_p0, device_id=target, device_id_type=MESH)
        p0.append((cond, copy))

        @pl.when(cond)
        def _():
            copy.start()

    sem = 0
    for tt in range(2):
        t = t0 + tt
        node = (t + SHIFT) % NODES
        slot = ka - (TILE * t) // OWN_ROWS
        cond = crosses if tt else ka >= 0
        for b in range(2):
            push0(cond, wplace.at[b, tt], rbuf.at[slot, ga], (node, b), sem)
            sem += 1
    for tt in range(2):
        t = t0 + tt
        node = (STRIPS + t % 8 + SHIFT) % NODES
        slot = ka - (TILE * t) // OWN_ROWS
        cond = jnp.logical_and(one, t < ANTI)
        if tt:
            cond = jnp.logical_and(cond, crosses)
        lanes = pl.ds(pl.multiple_of(jnp.minimum(t // 8, 6) * BLK, BLK), BLK)
        for b in range(2):
            push0(cond, wplace.at[b, tt, :, lanes], rbuf.at[slot, 1, :, lanes], (node, b), sem)
            sem += 1

    d_p = pltpu.make_async_remote_copy(pd, pfull.at[:, own_cols], s_d2d.at[0], r_d2d.at[0],
                                       device_id=sibling, device_id_type=MESH)
    d_p.start()
    d_q = pltpu.make_async_remote_copy(qsend, qfull.at[:, own_cols], s_d2d.at[1], r_d2d.at[1],
                                       device_id=sibling, device_id_type=MESH)
    d_q.start()

    @pl.when(is_strip)
    def _():
        pltpu.make_async_copy(rbuf, rbuf, r_p0).wait()
        half = [(rbuf[0, h].astype(F32) + rbuf[1, h].astype(F32)).astype(BF16) for h in range(2)]
        dbl[:, 0:HALF] = half[0]
        dbl[:, HALF:2 * HALF] = half[1]
        dbl[:, 2 * HALF:3 * HALF] = half[0]

    @pl.when(is_anti)
    def _():
        pltpu.make_async_copy(rbuf.at[:, 1], rbuf.at[:, 1], r_p0).wait()
        dbl[:, 0:HALF] = (rbuf[0, 1].astype(F32) + rbuf[1, 1].astype(F32)).astype(BF16)

    @pl.when(strip >= STRIPS + 8)
    def _():
        dbl[:, 0:HALF] = jnp.zeros((TILE, HALF), BF16)

    first = jnp.where(is_strip, strip // 8, 0)

    def window(j, n):
        return dbl[:, pl.ds(pl.multiple_of((first + j) * BLK, BLK), n * BLK)]

    m1[z, y, x, :, 0:128] = window(0, 1)
    m2[z, y, x] = window(1, 3)
    m1[z, y, x, :, 128:512] = window(4, 3)

    sends = []

    def push(src, target, ss, rs):
        copy = pltpu.make_async_remote_copy(src, src, ss, rs, device_id=target, device_id_type=MESH)
        copy.start()
        sends.append(copy)
        return copy

    c1 = []
    for d in (1, 2, 3):
        c1.append(push(m1.at[z, y, x], dev(dx=d), s_1.at[d - 1], r_1.at[d - 1]))
        c1.append(push(m2.at[z, y, x], dev(dy=d), s_1.at[d + 2], r_1.at[d + 2]))
    for c in c1:
        c.wait_recv()

    ca = [push(m1.at[z, y, :, :, pl.ds(0, 128)], dev(dy=d), s_a2.at[d - 1], r_a2.at[d - 1]) for d in (1, 2, 3)]

    def line_b(zp, xx):
        return m2.at[zp, :, xx]

    def line_c(zp, yy):
        return m1.at[zp, yy, :, :, pl.ds(128, 384)]

    def plane_a(zp):
        return m1.at[zp, :, :, :, pl.ds(0, 128)]

    zc = {}

    def z_send(dirn, dist, zp, kinds):
        g = 0 if dirn > 0 else 1
        got = zc.setdefault((g, dist), {})
        for kind in kinds:
            n = "abc".index(kind)
            if kind == "a":
                src = plane_a(zp) if dist < 4 else m1.at[zp, pl.ds(2 * g, 2), :, :, pl.ds(0, 128)]
            elif kind == "b":
                src = line_b(zp, x)
            else:
                src = line_c(zp, y)
            idx = (g * 4 + dist - 1) * 3 + n
            got[kind] = push(src, dev(dz=dirn), s_z.at[idx], r_z.at[idx])

    xy1, xy2 = {}, {}

    def xy_send(slot, zp):
        base = slot * 8
        xy1[slot] = [
            push(line_b(zp, x), dev(dx=1), s_xy.at[base], r_xy.at[base]),
            push(line_b(zp, x), dev(dx=-1), s_xy.at[base + 1], r_xy.at[base + 1]),
            push(line_c(zp, y), dev(dy=1), s_xy.at[base + 2], r_xy.at[base + 2]),
            push(line_c(zp, y), dev(dy=-1), s_xy.at[base + 3], r_xy.at[base + 3]),
        ]

    def xy_forward(slot, zp):
        base = slot * 8 + 4
        xl, xr = (x + 3) % NX, (x + 1) % NX
        yl, yr = (y + 3) % NY, (y + 1) % NY
        xy1[slot][0].wait_recv()
        f0 = push(m2.at[zp, pl.ds(0, 2), xl], dev(dx=1), s_xy.at[base], r_xy.at[base])
        xy1[slot][2].wait_recv()
        f2 = push(m1.at[zp, yl, pl.ds(0, 2), :, pl.ds(128, 384)], dev(dy=1), s_xy.at[base + 2], r_xy.at[base + 2])
        xy1[slot][1].wait_recv()
        f1 = push(m2.at[zp, pl.ds(2, 2), xr], dev(dx=-1), s_xy.at[base + 1], r_xy.at[base + 1])
        xy1[slot][3].wait_recv()
        f3 = push(m1.at[zp, yr, pl.ds(2, 2), :, pl.ds(128, 384)], dev(dy=-1), s_xy.at[base + 3], r_xy.at[base + 3])
        xy2[slot] = [f0, f1, f2, f3]

    def at(d):
        return (z + d + NZ) % NZ

    def blk(zp, h, j):
        if j == 0:
            v = m1[zp, 2 * h:2 * h + 2, :, :, 0:128]
        elif j <= 3:
            v = m2[zp, 2 * h:2 * h + 2, :, :, 128 * (j - 1):128 * j]
        else:
            v = m1[zp, 2 * h:2 * h + 2, :, :, 128 * (j - 3):128 * (j - 2)]
        return v.reshape(128, 128)

    def compute(zp):
        i = (zp + NZ - ZSHIFT) % NZ

        @pl.when(i < 7)
        def _():
            upper = blk(zp, 0, 1)
            wn[0:128, 0:128] = blk(zp, 0, 0)
            wn[0:128, 128:256] = upper
            wn[128:256, 0:128] = upper.astype(F32).T.astype(BF16)
            wn[128:256, 128:256] = blk(zp, 1, 0)
            for d in (1, 2, 3):
                wn[0:128, 256 * d:256 * d + 128] = blk(zp, 0, 2 * d)
                if d < 3:
                    wn[0:128, 256 * d + 128:256 * d + 256] = blk(zp, 0, 2 * d + 1)
                else:
                    wn[0:128, 256 * d + 128:256 * d + 256] = jnp.zeros((128, 128), BF16)
                wn[128:256, 256 * d:256 * d + 128] = blk(zp, 1, 2 * d - 1)
                wn[128:256, 256 * d + 128:256 * d + 256] = blk(zp, 1, 2 * d)

            @pl.loop(0, ROWS // MC)
            def _(m):
                rows = pl.ds(m * MC, MC)
                own = pfull[rows, pl.ds(pl.multiple_of(MXU * i, MXU), MXU)]
                for d in (1, 2, 3):
                    j = (i + d) % 7
                    acc[j, rows, :] += nn(own, wn[:, 256 * d:256 * d + 256])
                total = nn(own, wn[:, 0:256])
                for d in (1, 2, 3):
                    j = (i + d) % 7
                    cols = pl.ds(pl.multiple_of(MXU * j, MXU), MXU)
                    total += nt(pfull[rows, cols], wn[:, 256 * d:256 * d + 256])
                acc[i, rows, :] += total

        @pl.when(i == 7)
        def _():
            wn[:, 0:256] = jnp.zeros((256, 256), BF16)
            wn[:, 256:512] = jnp.zeros((256, 256), BF16)
            wn[:, 512:768] = jnp.zeros((256, 256), BF16)
            for b in range(3):
                wn[0:128, 256 * b:256 * b + 128] = blk(zp, 0, 2 * b)
                wn[128:256, 256 * b + 128:256 * b + 256] = blk(zp, 0, 2 * b + 1)
            wn[0:128, 768:896] = blk(zp, 0, 6)

            @pl.loop(0, ROWS // MC)
            def _(m):
                rows = pl.ds(m * MC, MC)
                for b in range(3):
                    w = wn[:, 256 * b:256 * b + 256]
                    r = nn(pfull[rows, 256 * b:256 * b + 256], w)
                    acc[3 + b, rows, 128:256] += r[:, 0:128]
                    acc[4 + b, rows, 0:128] += r[:, 128:256]
                    acc[b, rows, :] += nt(pfull[rows, 896 + 256 * b:896 + 256 * b + 256], w)
                w = wn[0:128, 768:896]
                acc[6, rows, 128:256] += nn(pfull[rows, 768:896], w)
                acc[3, rows, 0:128] += nt(pfull[rows, 1664:1792], w)

    slabs = {0: [(0, 0)], 1: [(1, -1), (2, 1)], 2: [(3, -2), (4, 2)], 3: [(5, -3), (6, 3)], 4: [(7, 4)]}
    z_send(1, 1, z, "bc")
    z_send(-1, 1, z, "bc")
    xy_send(0, z)
    for c in ca:
        c.wait_recv()
    z_send(1, 1, z, "a")
    z_send(-1, 1, z, "a")

    def arrive(dist):
        if dist < 4:
            for slot, delta in slabs[dist]:
                g = 0 if delta < 0 else 1
                dirn = 1 if delta < 0 else -1
                zp = at(delta)
                got = zc[(g, dist)]
                onward = "abc" if dist < 3 else ("ab" if g == 0 else "ac")
                for kind in "bca":
                    got[kind].wait_recv()
                    if kind in onward:
                        z_send(dirn, dist + 1, zp, kind)
                xy_send(slot, zp)
        else:
            zp = at(4)
            zc[(0, 4)]["b"].wait_recv()
            zc[(1, 4)]["c"].wait_recv()
            xy_send(7, zp)
            zc[(0, 4)]["a"].wait_recv()
            zc[(1, 4)]["a"].wait_recv()

    def forward(dist):
        for slot, delta in slabs[dist]:
            xy_forward(slot, at(delta))

    waited = []

    def finish(dist):
        for slot, delta in slabs[dist]:
            for c in xy2[slot]:
                c.wait_recv()
            if not waited:
                waited.append(1)
                l_pd.wait()
                d_p.wait_recv()
            compute(at(delta))

    arrive(1)
    forward(0)
    for dist in range(2, 5):
        arrive(dist)
        forward(dist - 1)
        finish(dist - 2)
    forward(4)
    finish(3)
    finish(4)

    d_q.wait_recv()

    @pl.loop(0, KP // 4)
    def _(a):
        rows = pl.ds(160 * a, 160)
        r = jnp.zeros((160, 160), F32)
        for b in range(7):
            r += nt(acc[b, rows, :].astype(BF16), qfull[rows, 256 * b:256 * b + 256])
        for h in range(4):
            kp[4 * a + h] = r[40 * h:40 * h + 40, 40 * h:40 * h + 40]

    live = cnt[...]
    for p in range(SLOTS):
        v = kp[:, p, :]
        mine[:, 40 * p:40 * p + 40] = jnp.where(live > p, v, 0.0)

    d_o = pltpu.make_async_remote_copy(mine, other, s_d2d.at[2], r_d2d.at[2], device_id=sibling, device_id_type=MESH)
    d_o.start()
    d_o.wait_recv()
    a, b = mine[...], other[...]
    for j in range(2):
        out[j] = jnp.where(qv[:, j:j + 1] == ga, a, b)

    d_o.wait_send()
    d_p.wait_send()
    d_q.wait_send()
    for c in sends:
        c.wait_send()
    for cond, copy in p0:
        @pl.when(cond)
        def _(copy=copy):
            copy.wait_send()


def local(pair_dens, counts, q_index, w_tiles, partner):
    wt = jnp.pad(jnp.transpose(w_tiles, (0, 2, 1)), ((0, 0), (0, TILE - OWN_ROWS), (0, 0)))
    anyspace = pl.BlockSpec(memory_space=pl.ANY)
    vmem = pl.BlockSpec(memory_space=pltpu.VMEM)
    smem = pl.BlockSpec(memory_space=pltpu.SMEM)
    dma = pltpu.SemaphoreType.DMA
    res = pl.pallas_call(
        kernel,
        out_shape=jax.ShapeDtypeStruct((2, KP, SLOTS * PC), F32),
        in_specs=[anyspace, anyspace, anyspace, vmem, vmem, smem],
        out_specs=vmem,
        scratch_shapes=[
            pltpu.VMEM((ROWS, NG), BF16),
            pltpu.VMEM((ROWS, NG), BF16),
            pltpu.VMEM((2 * ROWS, HALF), BF16),
            pltpu.VMEM((ROWS, HALF), BF16),
            pltpu.VMEM((NZ, NY, NX, TILE, 512), BF16),
            pltpu.VMEM((NZ, NY, NX, TILE, 384), BF16),
            pltpu.VMEM((7, ROWS, MXU), F32),
            pltpu.VMEM((2, 2, TILE, HALF), BF16),
            pltpu.VMEM((2, TILE, HALF), BF16),
            pltpu.VMEM((2, 2, TILE, HALF), BF16),
            pltpu.VMEM((TILE, 3 * HALF), BF16),
            pltpu.VMEM((MXU, 4 * MXU), BF16),
            pltpu.VMEM((KP, SLOTS, PC), F32),
            pltpu.VMEM((KP, SLOTS * PC), F32),
            pltpu.VMEM((KP, SLOTS * PC), F32),
            dma((3,)),
            dma((8,)), dma(()),
            dma((3,)), dma((3,)),
            dma((6,)), dma((6,)),
            dma((3,)), dma((3,)),
            dma((24,)), dma((24,)),
            dma((64,)), dma((64,)),
        ],
        compiler_params=pltpu.CompilerParams(
            collective_id=0, has_side_effects=True, vmem_limit_bytes=60 * 2**20),
        cost_estimate=pl.CostEstimate(flops=2 * ROWS * NG * NG, bytes_accessed=8 * 2**20, transcendentals=0),
    )(
        pair_dens.reshape(ROWS, HALF),
        partner.reshape(2 * ROWS, HALF),
        wt,
        counts.reshape(KP, 1),
        q_index,
        q_index.reshape(2 * KP),
    )
    return jnp.transpose(res, (1, 0, 2))


def solution(mesh):
    in_specs = (
        P("ka", None, "ga"),
        P("ka"),
        P("ka", None),
        P(None, "ga", "ka"),
        P("ka", None, None, "ga"),
    )
    return jax.shard_map(local, mesh=mesh, in_specs=in_specs, out_specs=P("ka", None, None), check_vma=False)
```

```python
import jax
import jax.numpy as jnp
from jax import lax
from jax.experimental import pallas as pl
from jax.experimental.pallas import tpu as pltpu
from jax.sharding import PartitionSpec as P

MESH = pl.DeviceIdType.MESH
BF16, F32 = jnp.bfloat16, jnp.float32

NX, NY, NZ = 4, 4, 8
NODES = NX * NY * NZ
KP, SLOTS, PC = 32, 40, 40
ROWS = KP * SLOTS
NG, HALF = 1792, 896
BLK, MXU = 128, 256
OWN_ROWS = NG // NODES
TILE = 16
STRIPS = NG // TILE
SLAB = NX * NY
WIN = 8
MC = 256


def nt(a, b):
    return lax.dot_general(a, b, (((1,), (1,)), ((), ())), preferred_element_type=F32)


def nn(a, b):
    return jnp.dot(a, b, preferred_element_type=F32)


def kernel(pd, part, wt, cnt_in, q_in, out,
           cnt, qs, pfull, qfull, praw, qsend, ma, mb, mc, acc, rbuf, wraw, wplace, wn, kp, mine, other,
           s_loc, s_p0, r_p0, s_d2d, r_d2d, s_1, r_1, s_a, r_a, s_z, r_z, s_xy, r_xy):
    ka = lax.axis_index("ka")
    ga = lax.axis_index("ga")
    x, y, z = ka % NX, (ka // NX) % NY, ka // (NX * NY)

    def dev(dz=0, dy=0, dx=0):
        return (((z + dz + NZ) % NZ) * (NX * NY) + ((y + dy + NY) % NY) * NX + (x + dx + NX) % NX, ga)

    sibling = (ka, 1 - ga)
    has_strip = ka < STRIPS

    bar = pltpu.get_barrier_semaphore()

    def greet(device):
        pl.semaphore_signal(bar, inc=1, device_id=device, device_id_type=MESH)

    i32 = lambda b: jnp.where(b, jnp.int32(1), jnp.int32(0))

    t0 = (OWN_ROWS * ka) // TILE
    off = (OWN_ROWS * ka) % TILE
    crosses = off + OWN_ROWS > TILE
    n_waits = jnp.int32(14)
    for d in (1, 2, 3):
        greet(dev(dx=d))
        greet(dev(dy=d))
    for d in range(1, NZ):
        greet(dev(dz=d))
    greet(sibling)

    first_src = (TILE * ka) // OWN_ROWS
    for a in range(2):
        for c in range(2):
            @pl.when(jnp.logical_and(has_strip, jnp.logical_or(first_src + a != ka, ga != c)))
            def _(a=a, c=c):
                greet((first_src + a, c))

    n_waits += (2 - i32(t0 == ka)) + i32(crosses) * (2 - i32(t0 + 1 == ka))

    own_cols = pl.ds(pl.multiple_of(ga * HALF, BLK), HALF)
    l_w = pltpu.make_async_copy(wt, wraw, s_loc.at[0])
    l_part = pltpu.make_async_copy(part, praw, s_loc.at[1])
    l_pd = pltpu.make_async_copy(pd, pfull.at[:, own_cols], s_loc.at[2])
    l_cnt = pltpu.make_async_copy(cnt_in, cnt, s_loc.at[3])
    l_q = pltpu.make_async_copy(q_in, qs, s_loc.at[4])
    l_w.start()
    l_cnt.start()
    l_q.start()
    l_part.start()
    l_pd.start()

    l_w.wait()
    row = lax.broadcasted_iota(jnp.int32, (2 * TILE, OWN_ROWS), 0)
    col = lax.broadcasted_iota(jnp.int32, (2 * TILE, OWN_ROWS), 1)
    place = jnp.where(row == col + off, 1.0, 0.0).astype(BF16)
    raw = wraw[...].astype(F32)
    for b in range(2):
        placed = nn(place, raw[:, b, :].astype(BF16)).astype(BF16)
        wplace[b, 0] = placed[:TILE]
        wplace[b, 1] = placed[TILE:]

    pl.semaphore_wait(bar, n_waits)

    p0 = []

    def push0(cond, src, dst, node, b, sem):
        copy = pltpu.make_async_remote_copy(src, dst, s_p0.at[sem], r_p0, device_id=(node, b), device_id_type=MESH)
        here = jnp.logical_and(node == ka, ga == b)
        away = jnp.logical_and(cond, jnp.logical_not(here))
        p0.append((away, copy))

        @pl.when(away)
        def _():
            copy.start()

        @pl.when(jnp.logical_and(cond, here))
        def _():
            pltpu.make_async_copy(src, dst, r_p0).start()

    sem = 0
    for tt in range(2):
        t = t0 + tt
        slot = ka - (TILE * t) // OWN_ROWS
        lead = (t // 8) % 7
        same = (t // 8) // 7 == ga
        start = jnp.where(same, lead, 0)
        shift = jnp.where(same, 0, 7 - lead)
        count = jnp.where(same, 7 - lead, lead + 1)
        for size in (4, 2, 1):
            cond = (count // size) % 2 == 1
            if tt:
                cond = jnp.logical_and(cond, crosses)
            more = (count // (2 * size)) * (2 * size)
            begin = jnp.minimum(start + more, 7 - size)
            to = jnp.minimum(shift + more, WIN - size)
            src = pl.ds(pl.multiple_of(begin * BLK, BLK), size * BLK)
            dst = pl.ds(pl.multiple_of(to * BLK, BLK), size * BLK)
            for b in range(2):
                push0(cond, wplace.at[b, tt, :, src], rbuf.at[slot, :, dst], t, b, sem)
                sem += 1

    d_p = pltpu.make_async_remote_copy(pd, pfull.at[:, own_cols], s_d2d.at[0], r_d2d.at[0],
                                       device_id=sibling, device_id_type=MESH)
    d_p.start()
    l_cnt.wait()
    l_q.wait()
    l_part.wait()

    @pl.loop(0, KP // 2)
    def _(kk):
        keep, send = [], []
        for h in range(2):
            k = 2 * kk + h
            both = praw[pl.ds(80 * k, 80), :].astype(F32)
            zero_first = qs[0, k] == ga
            keep.append(jnp.where(zero_first, both[:40], both[40:]))
            send.append(jnp.where(zero_first, both[40:], both[:40]))
        rows = pl.ds(80 * kk, 80)
        qfull[rows, own_cols] = jnp.concatenate(keep, axis=0).astype(BF16)
        qsend[rows, :] = jnp.concatenate(send, axis=0).astype(BF16)

    d_q = pltpu.make_async_remote_copy(qsend, qfull.at[:, own_cols], s_d2d.at[1], r_d2d.at[1],
                                       device_id=sibling, device_id_type=MESH)
    d_q.start()

    @pl.loop(0, ROWS // MC)
    def _(m):
        rows = pl.ds(m * MC, MC)
        for b in range(7):
            acc[b, rows, :] = jnp.zeros((MC, MXU), F32)

    @pl.when(has_strip)
    def _():
        pltpu.make_async_copy(rbuf, rbuf, r_p0).wait()
        whole = (rbuf[0].astype(F32) + rbuf[1].astype(F32)).astype(BF16)
        ma[z, y, x] = whole[:, 0:128]
        mb[z, y, x, :, 0:384] = whole[:, 128:512]
        mc[z, y, x] = whole[:, 512:896]
        mb[z, y, x, :, 384:512] = whole[:, 896:1024]

    sends = []

    def drain(sem, elements):
        lanes = 256 if elements > ROWS * 128 else 128
        ref = qsend.at[pl.ds(0, elements // lanes), pl.ds(0, lanes)]
        pltpu.make_async_copy(ref, ref, sem).wait()

    def push(zp, src, target, ss, rs):
        copy = pltpu.make_async_remote_copy(src, src, ss, rs, device_id=target, device_id_type=MESH)

        @pl.when(zp != NZ - 1)
        def _():
            copy.start()

    def arrive(zp, sem, elements):
        @pl.when(zp != NZ - 1)
        def _():
            drain(sem, elements)

    for d in (1, 2, 3):
        push(z, mb.at[z, y, x], dev(dy=d), s_1, r_1.at[0])
    for d in (1, 2, 3):
        push(z, mc.at[z, y, x], dev(dx=d), s_1, r_1.at[1])
    for d in range(1, NZ):
        push(z, ma.at[z, y, x], dev(dz=d), s_1, r_a.at[0])
    sends.append((z, s_1, TILE * (3 * 512 + 3 * 384 + 7 * 128)))

    B0, B1, C0 = 2 * TILE * 512, 2 * TILE * 384, 4 * TILE * 384

    def line_b(zp, xx, n):
        return mb.at[zp, pl.ds(0, 2), xx] if n == 0 else mb.at[zp, pl.ds(2, 2), xx, :, pl.ds(0, 384)]

    def z_send(g, dist, zp, kind):
        hop = (1 if dist < 4 else 2) * (1 if g == 0 else -1)
        srcs = [line_b(zp, x, 0), line_b(zp, x, 1)] if kind == "b" else [mc.at[zp, y]]
        n = g * 4 + dist - 1
        for src in srcs:
            push(zp, src, dev(dz=hop), s_z.at[n], r_z.at[2 * n + "bc".index(kind)])
        if dist < 4 and kind == "b":
            sends.append((zp, s_z.at[n], B0 + B1 + C0))
        elif dist == 4:
            sends.append((zp, s_z.at[n], B0 + B1 if kind == "b" else C0))

    def z_arrive(g, dist, zp, kind):
        arrive(zp, r_z.at[2 * (g * 4 + dist - 1) + "bc".index(kind)], B0 + B1 if kind == "b" else C0)

    def xy_send(slot, zp, kind):
        s, r = s_xy.at[slot], 5 * slot
        if kind == "b":
            push(zp, line_b(zp, x, 0), dev(dx=1), s, r_xy.at[r])
            push(zp, line_b(zp, x, 1), dev(dx=-1), s, r_xy.at[r + 1])
            push(zp, line_b(zp, x, 1), dev(dx=1), s, r_xy.at[r + 4])
            push(zp, line_b(zp, x, 0), dev(dx=-1), s, r_xy.at[r + 4])
        else:
            push(zp, mc.at[zp, y], dev(dy=1), s, r_xy.at[r + 2])
            push(zp, mc.at[zp, y], dev(dy=-1), s, r_xy.at[r + 3])
            sends.append((zp, s, 3 * (B0 + B1) + 3 * C0))

    def xy_forward(slot, zp):
        xl, xr = (x + 3) % NX, (x + 1) % NX
        yl, yr = (y + 3) % NY, (y + 1) % NY
        todo = [
            (B0, line_b(zp, xl, 0), dev(dx=1)),
            (B1, line_b(zp, xr, 1), dev(dx=-1)),
            (C0, mc.at[zp, yl, pl.ds(0, 2)], dev(dy=1)),
            (C0, mc.at[zp, yr, pl.ds(2, 2)], dev(dy=-1)),
        ]
        for n, (size, src, target) in enumerate(todo):
            arrive(zp, r_xy.at[5 * slot + n], size)
            push(zp, src, target, s_xy.at[slot], r_xy.at[5 * slot + 4])

    def at(d):
        return (z + d + NZ) % NZ

    SLOT = {0: 0, -1: 1, 1: 2, -2: 3, 2: 4, -3: 5, 3: 6, 4: 7}

    def z_step(dist, kind):
        if dist == 4:
            z_arrive(0 if kind == "b" else 1, 4, at(4), kind)
            xy_send(7, at(4), kind)
            return
        for g in (0, 1):
            delta = -dist if g == 0 else dist
            z_arrive(g, dist, at(delta), kind)
            if dist < 3:
                z_send(g, dist + 1, at(delta), kind)
            if dist == 2 and kind == "bc"[g]:
                z_send(g, 4, at(delta), kind)
            xy_send(SLOT[delta], at(delta), kind)

    def blk(zp, h, j):
        ref, lane = (ma, 0) if j == 0 else (mb, min(j - 1, 3)) if j <= 3 or j == 7 else (mc, j - 4)
        return ref[zp, 2 * h:2 * h + 2, :, :, 128 * lane:128 * lane + 128].reshape(128, 128)

    def compute(i):
        zp = i

        @pl.when(i < NZ - 1)
        def _():
            upper = blk(zp, 0, 1)
            wn[0:128, 0:128] = blk(zp, 0, 0)
            wn[0:128, 128:256] = upper
            wn[128:256, 0:128] = upper.astype(F32).T.astype(BF16)
            wn[128:256, 128:256] = blk(zp, 1, 0)
            for d in (1, 2, 3):
                wn[0:128, 256 * d:256 * d + 128] = blk(zp, 0, 2 * d)
                wn[0:128, 256 * d + 128:256 * d + 256] = blk(zp, 0, 2 * d + 1)
                wn[128:256, 256 * d:256 * d + 128] = blk(zp, 1, 2 * d - 1)
                wn[128:256, 256 * d + 128:256 * d + 256] = blk(zp, 1, 2 * d)

            own = pfull[:, pl.ds(pl.multiple_of(MXU * i, MXU), MXU)]
            for d in (1, 2, 3):
                acc[(i + d) % 7] += nn(own, wn[:, 256 * d:256 * d + 256])
            total = nn(own, wn[:, 0:256])
            for d in (1, 2, 3):
                cols = pl.ds(pl.multiple_of(MXU * ((i + d) % 7), MXU), MXU)
                total += nt(pfull[:, cols], wn[:, 256 * d:256 * d + 256])
            acc[i] += total

    def forward(dist):
        for delta in ((0,) if dist == 0 else (4,) if dist == 4 else (-dist, dist)):
            xy_forward(SLOT[delta], at(delta))

    def finish(dist):
        for delta in ((0,) if dist == 0 else (4,) if dist == 4 else (-dist, dist)):
            arrive(at(delta), r_xy.at[5 * SLOT[delta] + 4], 2 * (B0 + B1) + C0)
        if dist in (0, 4):
            compute(at(dist))
        else:
            @pl.loop(0, 2)
            def _(n):
                compute(at((2 * n - 1) * dist))

    arrive(z, r_1.at[0], 3 * TILE * 512)
    for g in (0, 1):
        z_send(g, 1, z, "b")
    xy_send(0, z, "b")
    arrive(z, r_1.at[1], 3 * TILE * 384)
    for g in (0, 1):
        z_send(g, 1, z, "c")
    xy_send(0, z, "c")

    A0 = 7 * TILE * 128

    def push_a(src, target, n, m):
        pltpu.make_async_remote_copy(src, src, s_a.at[n], r_a.at[m], device_id=target,
                                     device_id_type=MESH).start()

    @pl.when(z == NZ - 1)
    def _():
        drain(r_a.at[0], A0)

    @pl.when(z != NZ - 1)
    def _():
        drain(r_a.at[0], 6 * TILE * 128)

    for d in (1, 2, 3):
        push_a(ma.at[pl.ds(0, 7), y, x], dev(dx=d), 0, 1)
    z_step(1, "b")
    drain(r_a.at[1], 3 * A0)
    push_a(ma.at[pl.ds(0, 7), y], dev(dy=1), 1, 2)
    push_a(ma.at[pl.ds(0, 7), y], dev(dy=-1), 1, 3)
    z_step(1, "c")
    forward(0)
    z_step(2, "b")
    z_step(2, "c")
    drain(r_a.at[2], 4 * A0)
    push_a(ma.at[pl.ds(0, 7), (y + 3) % NY, pl.ds(0, 2)], dev(dy=1), 1, 4)
    drain(r_a.at[3], 4 * A0)
    push_a(ma.at[pl.ds(0, 7), (y + 1) % NY, pl.ds(2, 2)], dev(dy=-1), 1, 4)
    forward(1)
    z_step(3, "b")
    z_step(3, "c")
    z_step(4, "b")
    z_step(4, "c")
    drain(r_a.at[4], 4 * A0)
    l_pd.wait()
    d_p.wait_recv()
    finish(0)
    forward(2)
    finish(1)
    forward(3)
    forward(4)
    finish(2)
    finish(3)
    finish(4)

    d_q.wait_recv()

    @pl.loop(0, KP // 4, unroll=True)
    def _(a):
        rows = pl.ds(160 * a, 160)
        scr = jnp.concatenate([acc[b, rows, :].astype(BF16) for b in range(7)], axis=1)
        r = nt(scr, qfull[rows, :])
        for h in range(4):
            slot = lax.broadcasted_iota(jnp.int32, (SLOTS, PC), 0)
            block = r[40 * h:40 * h + 40, 40 * h:40 * h + 40]
            kp[4 * a + h] = jnp.where(slot < cnt[4 * a + h], block, 0.0)

    for p in range(SLOTS):
        mine[:, 40 * p:40 * p + 40] = kp[:, p, :]

    d_o = pltpu.make_async_remote_copy(mine, other, s_d2d.at[2], r_d2d.at[2], device_id=sibling, device_id_type=MESH)
    d_o.start()

    d_p.wait_send()
    d_q.wait_send()
    drain(s_a.at[0], 3 * A0)
    drain(s_a.at[1], 12 * A0)
    for zp, sem, elements in sends:
        arrive(zp, sem, elements)
    for cond, copy in p0:
        @pl.when(cond)
        def _(copy=copy):
            copy.wait_send()

    d_o.wait_recv()
    point = lax.broadcasted_iota(jnp.int32, (KP, 1), 0)
    first_tile = jnp.zeros((KP, 1), jnp.int32)
    for k in range(KP):
        first_tile = jnp.where(point == k, qs[0, k], first_tile)
    a, b = mine[...], other[...]
    out[0] = jnp.where(first_tile == ga, a, b)
    out[1] = jnp.where(first_tile == ga, b, a)
    d_o.wait_send()


def local(pair_dens, counts, q_index, w_tiles, partner):
    anyspace = pl.BlockSpec(memory_space=pl.ANY)
    vmem = pl.BlockSpec(memory_space=pltpu.VMEM)
    dma = pltpu.SemaphoreType.DMA
    res = pl.pallas_call(
        kernel,
        out_shape=jax.ShapeDtypeStruct((2, KP, SLOTS * PC), F32),
        in_specs=[anyspace] * 5,
        out_specs=vmem,
        scratch_shapes=[
            pltpu.SMEM((KP,), jnp.int32),
            pltpu.SMEM((2, KP), jnp.int32),
            pltpu.VMEM((ROWS, NG), BF16),
            pltpu.VMEM((ROWS, NG), BF16),
            pltpu.VMEM((2 * ROWS, HALF), BF16),
            pltpu.VMEM((ROWS, HALF), BF16),
            pltpu.VMEM((NZ, NY, NX, TILE, 128), BF16),
            pltpu.VMEM((NZ, NY, NX, TILE, 512), BF16),
            pltpu.VMEM((NZ, NY, NX, TILE, 384), BF16),
            pltpu.VMEM((7, ROWS, MXU), F32),
            pltpu.VMEM((2, TILE, WIN * BLK), BF16),
            pltpu.VMEM((OWN_ROWS, 2, HALF), BF16),
            pltpu.VMEM((2, 2, TILE, HALF), BF16),
            pltpu.VMEM((MXU, 4 * MXU), BF16),
            pltpu.VMEM((KP, SLOTS, PC), F32),
            pltpu.VMEM((KP, SLOTS * PC), F32),
            pltpu.VMEM((KP, SLOTS * PC), F32),
            dma((5,)),
            dma((12,)), dma(()),
            dma((3,)), dma((3,)),
            dma(()), dma((2,)),
            dma((2,)), dma((5,)),
            dma((8,)), dma((16,)),
            dma((8,)), dma((40,)),
        ],
        compiler_params=pltpu.CompilerParams(
            collective_id=0, has_side_effects=True, vmem_limit_bytes=60 * 2**20),
        cost_estimate=pl.CostEstimate(flops=2 * ROWS * NG * NG, bytes_accessed=8 * 2**20, transcendentals=0),
    )(
        pair_dens.reshape(ROWS, HALF),
        partner.reshape(2 * ROWS, HALF),
        jnp.transpose(w_tiles, (2, 0, 1)),
        counts,
        jnp.transpose(q_index),
    )
    return jnp.transpose(res, (1, 0, 2))


def solution(mesh):
    in_specs = (
        P("ka", None, "ga"),
        P("ka"),
        P("ka", None),
        P(None, "ga", "ka"),
        P("ka", None, None, "ga"),
    )
    return jax.shard_map(local, mesh=mesh, in_specs=in_specs, out_specs=P("ka", None, None), check_vma=False)
```

```python
import jax
import jax.numpy as jnp
from jax import lax
from jax.experimental import pallas as pl
from jax.experimental.pallas import tpu as pltpu
from jax.sharding import PartitionSpec as P

MESH = pl.DeviceIdType.MESH
BF16, F32 = jnp.bfloat16, jnp.float32

NX, NY, NZ = 4, 4, 8
NODES = NX * NY * NZ
KP, SLOTS, PC = 32, 40, 40
ROWS = KP * SLOTS
NG, HALF = 1792, 896
BLK, MXU = 128, 256
OWN_ROWS = NG // NODES
TILE = 16
STRIPS = NG // TILE
SLABS = 7
EMPTY = NZ // 2
WIN = 8
MC = 256


def nt(a, b):
    return lax.dot_general(a, b, (((1,), (1,)), ((), ())), preferred_element_type=F32)


def nn(a, b):
    return jnp.dot(a, b, preferred_element_type=F32)


def kernel(pd, part, wt, cnt_in, q_in, out,
           cnt, qs, pfull, qfull, praw, qsend, ma, mb, mc, acc, rbuf, wraw, wplace, wn, kp, mine, other,
           s_loc, s_p0, r_p0, s_d2d, r_d2d, s_1, r_1, s_a, r_a, s_z, r_z, s_xy, r_xy):
    ka = lax.axis_index("ka")
    ga = lax.axis_index("ga")
    z = ka // (NX * NY)
    x_here, y_here = ka % NX, (ka // NX) % NY
    u = jnp.where(ga == 0, x_here, y_here)
    v = jnp.where(ga == 0, y_here, x_here)

    def node_of(core, zz, vv, uu):
        return zz * (NX * NY) + jnp.where(core == 0, vv * NX + uu, uu * NX + vv)

    def dev(dz=0, dv=0, du=0):
        return (node_of(ga, (z + dz + NZ) % NZ, (v + dv + NY) % NY, (u + du + NX) % NX), ga)

    sibling = (ka, 1 - ga)
    i32 = lambda b: jnp.where(b, jnp.int32(1), jnp.int32(0))

    def slab_of(zp):
        return zp - i32(zp > EMPTY)

    def owner(t, core):
        slab = t // (NX * NY)
        return node_of(core, slab + i32(slab >= EMPTY), (t // NX) % NY, t % NX)

    has_strip = z != EMPTY
    me = slab_of(z)
    strip = me * (NX * NY) + v * NX + u

    bar = pltpu.get_barrier_semaphore()

    def greet(device):
        pl.semaphore_signal(bar, inc=1, device_id=device, device_id_type=MESH)

    t0 = (OWN_ROWS * ka) // TILE
    off = (OWN_ROWS * ka) % TILE
    crosses = off + OWN_ROWS > TILE
    n_waits = jnp.int32(26)
    for d in (1, 2, 3):
        for dz in (0, -1, 1):
            greet(dev(dz, 0, d))
            greet(dev(dz, d, 0))
    for d in range(1, NZ):
        greet(dev(dz=d))
    greet(sibling)

    first_src = (TILE * strip) // OWN_ROWS
    for a in range(2):
        for c in range(2):
            @pl.when(jnp.logical_and(has_strip, jnp.logical_or(first_src + a != ka, ga != c)))
            def _(a=a, c=c):
                greet((first_src + a, c))

    n_waits += (2 - i32(owner(t0, ga) == ka)) + i32(crosses) * (2 - i32(owner(t0 + 1, ga) == ka))

    own_cols = pl.ds(pl.multiple_of(ga * HALF, BLK), HALF)
    l_w = pltpu.make_async_copy(wt, wraw, s_loc.at[0])
    l_part = pltpu.make_async_copy(part, praw, s_loc.at[1])
    l_pd = pltpu.make_async_copy(pd, pfull.at[:, own_cols], s_loc.at[2])
    l_cnt = pltpu.make_async_copy(cnt_in, cnt, s_loc.at[3])
    l_q = pltpu.make_async_copy(q_in, qs, s_loc.at[4])
    l_w.start()
    l_cnt.start()
    l_q.start()
    l_part.start()
    l_pd.start()

    l_w.wait()
    row = lax.broadcasted_iota(jnp.int32, (2 * TILE, OWN_ROWS), 0)
    col = lax.broadcasted_iota(jnp.int32, (2 * TILE, OWN_ROWS), 1)
    place = jnp.where(row == col + off, 1.0, 0.0).astype(BF16)
    raw = wraw[...].astype(F32)
    for b in range(2):
        placed = nn(place, raw[:, b, :].astype(BF16)).astype(BF16)
        wplace[b, 0] = placed[:TILE]
        wplace[b, 1] = placed[TILE:]

    pl.semaphore_wait(bar, n_waits)

    p0 = []

    def push0(cond, src, dst, node, b, sem):
        copy = pltpu.make_async_remote_copy(src, dst, s_p0.at[sem], r_p0, device_id=(node, b), device_id_type=MESH)
        here = jnp.logical_and(node == ka, ga == b)
        away = jnp.logical_and(cond, jnp.logical_not(here))
        p0.append((away, copy))

        @pl.when(away)
        def _():
            copy.start()

        @pl.when(jnp.logical_and(cond, here))
        def _():
            pltpu.make_async_copy(src, dst, r_p0).start()

    sem = 0
    for tt in range(2):
        t = t0 + tt
        slot = ka - (TILE * t) // OWN_ROWS
        lead = (t // 8) % 7
        same = (t // 8) // 7 == ga
        start = jnp.where(same, lead, 0)
        shift = jnp.where(same, 0, 7 - lead)
        count = jnp.where(same, 7 - lead, lead + 1)
        for size in (4, 2, 1):
            cond = (count // size) % 2 == 1
            if tt:
                cond = jnp.logical_and(cond, crosses)
            more = (count // (2 * size)) * (2 * size)
            begin = jnp.minimum(start + more, 7 - size)
            to = jnp.minimum(shift + more, WIN - size)
            src = pl.ds(pl.multiple_of(begin * BLK, BLK), size * BLK)
            dst = pl.ds(pl.multiple_of(to * BLK, BLK), size * BLK)
            for b in range(2):
                push0(cond, wplace.at[b, tt, :, src], rbuf.at[slot, :, dst], owner(t, b), b, sem)
                sem += 1

    d_p = pltpu.make_async_remote_copy(pd, pfull.at[:, own_cols], s_d2d.at[0], r_d2d.at[0],
                                       device_id=sibling, device_id_type=MESH)
    d_p.start()
    l_cnt.wait()
    l_q.wait()
    l_part.wait()

    @pl.loop(0, KP // 2)
    def _(kk):
        keep, send = [], []
        for h in range(2):
            k = 2 * kk + h
            both = praw[pl.ds(80 * k, 80), :].astype(F32)
            zero_first = qs[0, k] == ga
            keep.append(jnp.where(zero_first, both[:40], both[40:]))
            send.append(jnp.where(zero_first, both[40:], both[:40]))
        rows = pl.ds(80 * kk, 80)
        qfull[rows, own_cols] = jnp.concatenate(keep, axis=0).astype(BF16)
        qsend[rows, :] = jnp.concatenate(send, axis=0).astype(BF16)

    d_q = pltpu.make_async_remote_copy(qsend, qfull.at[:, own_cols], s_d2d.at[1], r_d2d.at[1],
                                       device_id=sibling, device_id_type=MESH)
    d_q.start()

    @pl.loop(0, ROWS // MC)
    def _(m):
        rows = pl.ds(m * MC, MC)
        for b in range(7):
            acc[b, rows, :] = jnp.zeros((MC, MXU), F32)

    @pl.when(has_strip)
    def _():
        pltpu.make_async_copy(rbuf, rbuf, r_p0).wait()
        whole = (rbuf[0].astype(F32) + rbuf[1].astype(F32)).astype(BF16)
        ma[me, v, u] = whole[:, 0:128]
        mb[me, v, u, :, 0:384] = whole[:, 128:512]
        mc[me, v, u] = whole[:, 512:896]
        mb[me, v, u, :, 384:512] = whole[:, 896:1024]

    sends = []

    def drain(sem, elements):
        lanes = 128 if elements <= ROWS * 128 else 256 if elements <= ROWS * 256 else HALF
        ref = qsend.at[pl.ds(0, elements // lanes), pl.ds(0, lanes)]
        pltpu.make_async_copy(ref, ref, sem).wait()

    def push(zp, src, target, ss, rs):
        copy = pltpu.make_async_remote_copy(src, src, ss, rs, device_id=target, device_id_type=MESH)

        @pl.when(zp != EMPTY)
        def _():
            copy.start()

    def arrive(zp, sem, elements):
        @pl.when(zp != EMPTY)
        def _():
            drain(sem, elements)

    for d in (1, 2, 3):
        push(z, mb.at[me, v, u], dev(dv=d), s_1, r_1.at[0])
    for d in (1, 2, 3):
        push(z, mc.at[me, v, u], dev(du=d), s_1, r_1.at[1])
    for d in range(1, NZ):
        push(z, ma.at[me, v, u], dev(dz=d), s_1, r_a.at[0])
    for g, dz in ((0, 1), (1, -1)):
        for d in range(4):
            push(z, mb.at[me, v, u], dev(dz, d, 0), s_1, r_z.at[8 * g])
    for g, dz in ((0, 1), (1, -1)):
        for d in range(4):
            push(z, mc.at[me, v, u], dev(dz, 0, d), s_1, r_z.at[8 * g + 1])
    sends.append((z, s_1, TILE * (11 * 512 + 11 * 384 + 7 * 128)))

    B0, B1, C0 = 2 * TILE * 512, 2 * TILE * 384, 4 * TILE * 384

    def line_b(zp, uu, n):
        return mb.at[slab_of(zp), pl.ds(0, 2), uu] if n == 0 else mb.at[slab_of(zp), pl.ds(2, 2), uu, :, pl.ds(0, 384)]

    def z_send(g, dist, zp, kind):
        hop = (1 if dist < 4 else 2) * (1 if g == 0 else -1)
        srcs = [line_b(zp, u, 0), line_b(zp, u, 1)] if kind == "b" else [mc.at[slab_of(zp), v]]
        n = g * 4 + dist - 1
        for src in srcs:
            push(zp, src, dev(dz=hop), s_z.at[n], r_z.at[2 * n + "bc".index(kind)])
        if dist < 4 and kind == "b":
            sends.append((zp, s_z.at[n], B0 + B1 + C0))
        elif dist == 4:
            sends.append((zp, s_z.at[n], B0 + B1 if kind == "b" else C0))

    def z_arrive(g, dist, zp, kind):
        if dist == 1:
            arrive(zp, r_z.at[8 * g + "bc".index(kind)], 4 * TILE * (512 if kind == "b" else 384))
            return
        arrive(zp, r_z.at[2 * (g * 4 + dist - 1) + "bc".index(kind)], B0 + B1 if kind == "b" else C0)

    def xy_send(slot, zp, kind):
        s, r = s_xy, 5 * slot
        if kind == "b":
            push(zp, line_b(zp, u, 0), dev(du=1), s, r_xy.at[r])
            push(zp, line_b(zp, u, 1), dev(du=-1), s, r_xy.at[r + 1])
            push(zp, line_b(zp, u, 1), dev(du=1), s, r_xy.at[r + 4])
            push(zp, line_b(zp, u, 0), dev(du=-1), s, r_xy.at[r + 4])
        else:
            push(zp, mc.at[slab_of(zp), v], dev(dv=1), s, r_xy.at[r + 2])
            push(zp, mc.at[slab_of(zp), v], dev(dv=-1), s, r_xy.at[r + 3])

    def xy_forward(slot, zp):
        ul, ur = (u + 3) % NX, (u + 1) % NX
        vl, vr = (v + 3) % NY, (v + 1) % NY
        todo = [
            (B0, line_b(zp, ul, 0), dev(du=1)),
            (B1, line_b(zp, ur, 1), dev(du=-1)),
            (C0, mc.at[slab_of(zp), vl, pl.ds(0, 2)], dev(dv=1)),
            (C0, mc.at[slab_of(zp), vr, pl.ds(2, 2)], dev(dv=-1)),
        ]
        for n, (size, src, target) in enumerate(todo):
            arrive(zp, r_xy.at[5 * slot + n], size)
            push(zp, src, target, s_xy, r_xy.at[5 * slot + 4])

    def at(d):
        return (z + d + NZ) % NZ

    SLOT = {0: 0, -1: 1, 1: 2, -2: 3, 2: 4, -3: 5, 3: 6, 4: 7}

    def z_step(dist, kind):
        if dist == 4:
            z_arrive(0 if kind == "b" else 1, 4, at(4), kind)
            xy_send(7, at(4), kind)
            return
        for g in (0, 1):
            delta = -dist if g == 0 else dist
            z_arrive(g, dist, at(delta), kind)
            if dist < 3:
                z_send(g, dist + 1, at(delta), kind)
            if dist == 2 and kind == "bc"[g]:
                z_send(g, 4, at(delta), kind)
            xy_send(SLOT[delta], at(delta), kind)

    def blk(zp, h, j):
        ref, lane = (ma, 0) if j == 0 else (mb, min(j - 1, 3)) if j <= 3 or j == 7 else (mc, j - 4)
        return ref[zp, 2 * h:2 * h + 2, :, :, 128 * lane:128 * lane + 128].reshape(128, 128)

    def own_rows(i):
        return pfull[:, pl.ds(pl.multiple_of(MXU * i, MXU), MXU)]

    def set_diagonal(i):
        upper = blk(i, 0, 1)
        wn[0:128, 0:128] = blk(i, 0, 0)
        wn[0:128, 128:256] = upper
        wn[128:256, 0:128] = upper.astype(F32).T.astype(BF16)
        wn[128:256, 128:256] = blk(i, 1, 0)

    def compute(zp, whole):
        i = slab_of(zp)

        @pl.when(zp != EMPTY)
        def _():
            if whole:
                set_diagonal(i)
            for d in (1, 2, 3):
                wn[0:128, 256 * d:256 * d + 128] = blk(i, 0, 2 * d)
                wn[0:128, 256 * d + 128:256 * d + 256] = blk(i, 0, 2 * d + 1)
                wn[128:256, 256 * d:256 * d + 128] = blk(i, 1, 2 * d - 1)
                wn[128:256, 256 * d + 128:256 * d + 256] = blk(i, 1, 2 * d)
            own = own_rows(i)
            for d in (1, 2, 3):
                acc[(i + d) % 7] += nn(own, wn[:, 256 * d:256 * d + 256])
            total = nt(own_rows((i + 1) % 7), wn[:, 256:512])
            for d in (2, 3):
                total += nt(own_rows((i + d) % 7), wn[:, 256 * d:256 * d + 256])
            if whole:
                total += nn(own, wn[:, 0:256])
            acc[i] += total

    def diagonals():
        @pl.loop(0, 3)
        def _(n):
            i = slab_of(at(n - 1))

            @pl.when(at(n - 1) != EMPTY)
            def _():
                set_diagonal(i)
                acc[i] += nn(own_rows(i), wn[:, 0:256])

    def forward(dist):
        for delta in ((0,) if dist == 0 else (4,) if dist == 4 else (-dist, dist)):
            xy_forward(SLOT[delta], at(delta))

    def finish(dist):
        for delta in ((0,) if dist == 0 else (4,) if dist == 4 else (-dist, dist)):
            arrive(at(delta), r_xy.at[5 * SLOT[delta] + 4], 2 * (B0 + B1) + C0)
        if dist in (0, 4):
            compute(at(dist), dist > 1)
        else:
            @pl.loop(0, 2)
            def _(n):
                compute(at((2 * n - 1) * dist), dist > 1)

    arrive(z, r_1.at[0], 3 * TILE * 512)
    xy_send(0, z, "b")
    arrive(z, r_1.at[1], 3 * TILE * 384)
    xy_send(0, z, "c")

    A0 = 7 * TILE * 128

    def push_a(src, target, n, m):
        pltpu.make_async_remote_copy(src, src, s_a.at[n], r_a.at[m], device_id=target,
                                     device_id_type=MESH).start()

    @pl.when(z == EMPTY)
    def _():
        drain(r_a.at[0], A0)

    @pl.when(z != EMPTY)
    def _():
        drain(r_a.at[0], 6 * TILE * 128)

    for d in (1, 2, 3):
        push_a(ma.at[:, v, u], dev(du=d), 0, 1)
    z_step(1, "b")
    z_step(1, "c")
    forward(0)
    z_step(2, "b")
    z_step(2, "c")
    drain(r_a.at[1], 3 * A0)
    push_a(ma.at[:, v], dev(dv=1), 1, 2)
    push_a(ma.at[:, v], dev(dv=-1), 1, 3)
    forward(1)
    z_step(3, "b")
    z_step(3, "c")
    z_step(4, "b")
    z_step(4, "c")
    l_pd.wait()
    d_p.wait_recv()
    finish(0)
    forward(2)
    drain(r_a.at[2], 4 * A0)
    push_a(ma.at[:, (v + 3) % NY, pl.ds(0, 2)], dev(dv=1), 1, 4)
    drain(r_a.at[3], 4 * A0)
    push_a(ma.at[:, (v + 1) % NY, pl.ds(2, 2)], dev(dv=-1), 1, 4)
    finish(1)
    forward(3)
    forward(4)
    drain(r_a.at[4], 4 * A0)
    diagonals()
    finish(2)
    finish(3)
    finish(4)

    d_q.wait_recv()

    @pl.loop(0, KP // 4, unroll=True)
    def _(a):
        rows = pl.ds(160 * a, 160)
        scr = jnp.concatenate([acc[b, rows, :].astype(BF16) for b in range(7)], axis=1)
        r = nt(scr, qfull[rows, :])
        for h in range(4):
            slot = lax.broadcasted_iota(jnp.int32, (SLOTS, PC), 0)
            block = r[40 * h:40 * h + 40, 40 * h:40 * h + 40]
            kp[4 * a + h] = jnp.where(slot < cnt[4 * a + h], block, 0.0)

    for p in range(SLOTS):
        mine[:, 40 * p:40 * p + 40] = kp[:, p, :]

    d_o = pltpu.make_async_remote_copy(mine, other, s_d2d.at[2], r_d2d.at[2], device_id=sibling, device_id_type=MESH)
    d_o.start()

    d_p.wait_send()
    d_q.wait_send()
    drain(s_a.at[0], 3 * A0)
    drain(s_a.at[1], 12 * A0)
    drain(s_xy, SLABS * 3 * (B0 + B1 + C0))
    for zp, sem, elements in sends:
        arrive(zp, sem, elements)
    for cond, copy in p0:
        @pl.when(cond)
        def _(copy=copy):
            copy.wait_send()

    d_o.wait_recv()
    point = lax.broadcasted_iota(jnp.int32, (KP, 1), 0)
    first_tile = jnp.zeros((KP, 1), jnp.int32)
    for k in range(KP):
        first_tile = jnp.where(point == k, qs[0, k], first_tile)
    a, b = mine[...], other[...]
    out[0] = jnp.where(first_tile == ga, a, b)
    out[1] = jnp.where(first_tile == ga, b, a)
    d_o.wait_send()


def local(pair_dens, counts, q_index, w_tiles, partner):
    anyspace = pl.BlockSpec(memory_space=pl.ANY)
    vmem = pl.BlockSpec(memory_space=pltpu.VMEM)
    dma = pltpu.SemaphoreType.DMA
    res = pl.pallas_call(
        kernel,
        out_shape=jax.ShapeDtypeStruct((2, KP, SLOTS * PC), F32),
        in_specs=[anyspace] * 5,
        out_specs=vmem,
        scratch_shapes=[
            pltpu.SMEM((KP,), jnp.int32),
            pltpu.SMEM((2, KP), jnp.int32),
            pltpu.VMEM((ROWS, NG), BF16),
            pltpu.VMEM((ROWS, NG), BF16),
            pltpu.VMEM((2 * ROWS, HALF), BF16),
            pltpu.VMEM((ROWS, HALF), BF16),
            pltpu.VMEM((SLABS, NY, NX, TILE, 128), BF16),
            pltpu.VMEM((SLABS, NY, NX, TILE, 512), BF16),
            pltpu.VMEM((SLABS, NY, NX, TILE, 384), BF16),
            pltpu.VMEM((7, ROWS, MXU), F32),
            pltpu.VMEM((2, TILE, WIN * BLK), BF16),
            pltpu.VMEM((OWN_ROWS, 2, HALF), BF16),
            pltpu.VMEM((2, 2, TILE, HALF), BF16),
            pltpu.VMEM((MXU, 4 * MXU), BF16),
            pltpu.VMEM((KP, SLOTS, PC), F32),
            pltpu.VMEM((KP, SLOTS * PC), F32),
            pltpu.VMEM((KP, SLOTS * PC), F32),
            dma((5,)),
            dma((12,)), dma(()),
            dma((3,)), dma((3,)),
            dma(()), dma((2,)),
            dma((2,)), dma((5,)),
            dma((8,)), dma((16,)),
            dma(()), dma((40,)),
        ],
        compiler_params=pltpu.CompilerParams(
            collective_id=0, has_side_effects=True, vmem_limit_bytes=60 * 2**20),
        cost_estimate=pl.CostEstimate(flops=2 * ROWS * NG * NG, bytes_accessed=8 * 2**20, transcendentals=0),
    )(
        pair_dens.reshape(ROWS, HALF),
        partner.reshape(2 * ROWS, HALF),
        jnp.transpose(w_tiles, (2, 0, 1)),
        counts,
        jnp.transpose(q_index),
    )
    return jnp.transpose(res, (1, 0, 2))


def solution(mesh):
    in_specs = (
        P("ka", None, "ga"),
        P("ka"),
        P("ka", None),
        P(None, "ga", "ka"),
        P("ka", None, None, "ga"),
    )
    return jax.shard_map(local, mesh=mesh, in_specs=in_specs, out_specs=P("ka", None, None), check_vma=False)
```

```python
import jax
import jax.numpy as jnp
from jax import lax
from jax.experimental import pallas as pl
from jax.experimental.pallas import tpu as pltpu
from jax.sharding import PartitionSpec as P

MESH = pl.DeviceIdType.MESH
BF16, F32 = jnp.bfloat16, jnp.float32

NX, NY, NZ = 4, 4, 8
NODES = NX * NY * NZ
KP, SLOTS, PC = 32, 40, 40
ROWS = KP * SLOTS
NG, HALF = 1792, 896
BLK, MXU = 128, 256
OWN_ROWS = NG // NODES
TILE = 16
STRIPS = NG // TILE
SLABS = 7
EMPTY = NZ // 2
WIN = 8
MC = 256


def nt(a, b):
    return lax.dot_general(a, b, (((1,), (1,)), ((), ())), preferred_element_type=F32)


def nn(a, b):
    return jnp.dot(a, b, preferred_element_type=F32)


def kernel(pd, part, wt, cnt_in, q_in, out,
           cnt, qs, pfull, qfull, praw, qsend, ma, mb, mc, acc, rbuf, wraw, wplace, wn, kp, mine, other,
           s_loc, s_p0, r_p0, s_d2d, r_d2d, s_1, r_1, s_a, r_a, s_z, r_z, s_xy, r_xy):
    ka = lax.axis_index("ka")
    ga = lax.axis_index("ga")
    z = ka // (NX * NY)
    x_here, y_here = ka % NX, (ka // NX) % NY
    u = jnp.where(ga == 0, x_here, y_here)
    v = jnp.where(ga == 0, y_here, x_here)

    def node_of(core, zz, vv, uu):
        return zz * (NX * NY) + jnp.where(core == 0, vv * NX + uu, uu * NX + vv)

    def dev(dz=0, dv=0, du=0):
        return (node_of(ga, (z + dz + NZ) % NZ, (v + dv + NY) % NY, (u + du + NX) % NX), ga)

    sibling = (ka, 1 - ga)
    i32 = lambda b: jnp.where(b, jnp.int32(1), jnp.int32(0))

    def slab_of(zp):
        return zp - i32(zp > EMPTY)

    def owner(t, core):
        slab = t // (NX * NY)
        return node_of(core, slab + i32(slab >= EMPTY), (t // NX) % NY, t % NX)

    has_strip = z != EMPTY
    me = slab_of(z)
    strip = me * (NX * NY) + v * NX + u

    bar = pltpu.get_barrier_semaphore()

    def greet(device):
        pl.semaphore_signal(bar, inc=1, device_id=device, device_id_type=MESH)

    t0 = (OWN_ROWS * ka) // TILE
    off = (OWN_ROWS * ka) % TILE
    crosses = off + OWN_ROWS > TILE
    n_waits = jnp.int32(26)
    for d in (1, 2, 3):
        for dz in (0, -1, 1):
            greet(dev(dz, 0, d))
            greet(dev(dz, d, 0))
    for d in range(1, NZ):
        greet(dev(dz=d))
    greet(sibling)

    first_src = (TILE * strip) // OWN_ROWS
    for a in range(2):
        for c in range(2):
            @pl.when(jnp.logical_and(has_strip, jnp.logical_or(first_src + a != ka, ga != c)))
            def _(a=a, c=c):
                greet((first_src + a, c))

    n_waits += (2 - i32(owner(t0, ga) == ka)) + i32(crosses) * (2 - i32(owner(t0 + 1, ga) == ka))

    own_cols = pl.ds(pl.multiple_of(ga * HALF, BLK), HALF)
    l_w = pltpu.make_async_copy(wt, wraw, s_loc.at[0])
    l_part = pltpu.make_async_copy(part, praw, s_loc.at[1])
    l_pd = pltpu.make_async_copy(pd, pfull.at[:, own_cols], s_loc.at[2])
    l_cnt = pltpu.make_async_copy(cnt_in, cnt, s_loc.at[3])
    l_q = pltpu.make_async_copy(q_in, qs, s_loc.at[4])
    l_w.start()
    l_cnt.start()
    l_q.start()
    l_part.start()
    l_pd.start()

    l_w.wait()
    row = lax.broadcasted_iota(jnp.int32, (2 * TILE, OWN_ROWS), 0)
    col = lax.broadcasted_iota(jnp.int32, (2 * TILE, OWN_ROWS), 1)
    place = jnp.where(row == col + off, 1.0, 0.0).astype(BF16)
    raw = wraw[...].astype(F32)
    for b in range(2):
        placed = nn(place, raw[:, b, :].astype(BF16)).astype(BF16)
        wplace[b, 0] = placed[:TILE]
        wplace[b, 1] = placed[TILE:]

    pl.semaphore_wait(bar, n_waits)

    p0 = []

    def push0(cond, src, dst, node, b, sem):
        copy = pltpu.make_async_remote_copy(src, dst, s_p0.at[sem], r_p0, device_id=(node, b), device_id_type=MESH)
        here = jnp.logical_and(node == ka, ga == b)
        away = jnp.logical_and(cond, jnp.logical_not(here))
        p0.append((away, copy))

        @pl.when(away)
        def _():
            copy.start()

        @pl.when(jnp.logical_and(cond, here))
        def _():
            pltpu.make_async_copy(src, dst, r_p0).start()

    sem = 0
    for tt in range(2):
        t = t0 + tt
        slot = ka - (TILE * t) // OWN_ROWS
        lead = (t // 8) % 7
        same = (t // 8) // 7 == ga
        start = jnp.where(same, lead, 0)
        shift = jnp.where(same, 0, 7 - lead)
        count = jnp.where(same, 7 - lead, lead + 1)
        for size in (4, 2, 1):
            cond = (count // size) % 2 == 1
            if tt:
                cond = jnp.logical_and(cond, crosses)
            more = (count // (2 * size)) * (2 * size)
            begin = jnp.minimum(start + more, 7 - size)
            to = jnp.minimum(shift + more, WIN - size)
            src = pl.ds(pl.multiple_of(begin * BLK, BLK), size * BLK)
            dst = pl.ds(pl.multiple_of(to * BLK, BLK), size * BLK)
            for b in range(2):
                push0(cond, wplace.at[b, tt, :, src], rbuf.at[slot, :, dst], owner(t, b), b, sem)
                sem += 1

    d_p = pltpu.make_async_remote_copy(pd, pfull.at[:, own_cols], s_d2d.at[0], r_d2d.at[0],
                                       device_id=sibling, device_id_type=MESH)
    d_p.start()
    l_cnt.wait()
    l_q.wait()
    l_part.wait()

    @pl.loop(0, KP // 2)
    def _(kk):
        keep, send = [], []
        for h in range(2):
            k = 2 * kk + h
            both = praw[pl.ds(80 * k, 80), :].astype(F32)
            zero_first = qs[0, k] == ga
            keep.append(jnp.where(zero_first, both[:40], both[40:]))
            send.append(jnp.where(zero_first, both[40:], both[:40]))
        rows = pl.ds(80 * kk, 80)
        qfull[rows, own_cols] = jnp.concatenate(keep, axis=0).astype(BF16)
        qsend[rows, :] = jnp.concatenate(send, axis=0).astype(BF16)

    d_q = pltpu.make_async_remote_copy(qsend, qfull.at[:, own_cols], s_d2d.at[1], r_d2d.at[1],
                                       device_id=sibling, device_id_type=MESH)
    d_q.start()

    @pl.loop(0, ROWS // MC)
    def _(m):
        rows = pl.ds(m * MC, MC)
        for b in range(7):
            acc[b, rows, :] = jnp.zeros((MC, MXU), F32)

    @pl.when(has_strip)
    def _():
        pltpu.make_async_copy(rbuf, rbuf, r_p0).wait()
        whole = (rbuf[0].astype(F32) + rbuf[1].astype(F32)).astype(BF16)
        ma[me, v, u] = whole[:, 0:128]
        mb[me, v, u, :, 0:384] = whole[:, 128:512]
        mc[me, v, u] = whole[:, 512:896]
        mb[me, v, u, :, 384:512] = whole[:, 896:1024]

    sends = []

    def drain(sem, elements):
        lanes = 128 if elements <= ROWS * 128 else 256 if elements <= ROWS * 256 else HALF
        ref = qsend.at[pl.ds(0, elements // lanes), pl.ds(0, lanes)]
        pltpu.make_async_copy(ref, ref, sem).wait()

    def push(zp, src, target, ss, rs):
        copy = pltpu.make_async_remote_copy(src, src, ss, rs, device_id=target, device_id_type=MESH)

        @pl.when(zp != EMPTY)
        def _():
            copy.start()

    def arrive(zp, sem, elements):
        @pl.when(zp != EMPTY)
        def _():
            drain(sem, elements)

    for d in (1, 2, 3):
        push(z, mb.at[me, v, u], dev(dv=d), s_1, r_1.at[0])
    for d in (1, 2, 3):
        push(z, mc.at[me, v, u], dev(du=d), s_1, r_1.at[1])
    for d in range(1, NZ):
        push(z, ma.at[me, v, u], dev(dz=d), s_1, r_a.at[0])
    for g, dz in ((0, 1), (1, -1)):
        for d in range(4):
            push(z, mb.at[me, v, u], dev(dz, d, 0), s_1, r_z.at[8 * g])
    for g, dz in ((0, 1), (1, -1)):
        for d in range(4):
            push(z, mc.at[me, v, u], dev(dz, 0, d), s_1, r_z.at[8 * g + 1])
    sends.append((z, s_1, TILE * (11 * 512 + 11 * 384 + 7 * 128)))

    B0, B1, C0 = 2 * TILE * 512, 2 * TILE * 384, 4 * TILE * 384

    def line_b(zp, uu, n):
        return mb.at[slab_of(zp), pl.ds(0, 2), uu] if n == 0 else mb.at[slab_of(zp), pl.ds(2, 2), uu, :, pl.ds(0, 384)]

    def z_send(g, dist, zp, kind):
        hop = (1 if dist < 4 else 2) * (1 if g == 0 else -1)
        srcs = [line_b(zp, u, 0), line_b(zp, u, 1)] if kind == "b" else [mc.at[slab_of(zp), v]]
        n = g * 4 + dist - 1
        for src in srcs:
            push(zp, src, dev(dz=hop), s_z.at[n], r_z.at[2 * n + "bc".index(kind)])
        if dist < 4 and kind == "b":
            sends.append((zp, s_z.at[n], B0 + B1 + C0))
        elif dist == 4:
            sends.append((zp, s_z.at[n], B0 + B1 if kind == "b" else C0))

    def z_arrive(g, dist, zp, kind):
        if dist == 1:
            arrive(zp, r_z.at[8 * g + "bc".index(kind)], 4 * TILE * (512 if kind == "b" else 384))
            return
        arrive(zp, r_z.at[2 * (g * 4 + dist - 1) + "bc".index(kind)], B0 + B1 if kind == "b" else C0)

    def xy_send(slot, zp, kind):
        s, r = s_xy, 5 * slot
        if kind == "b":
            push(zp, line_b(zp, u, 0), dev(du=1), s, r_xy.at[r])
            push(zp, line_b(zp, u, 1), dev(du=-1), s, r_xy.at[r + 1])
            push(zp, line_b(zp, u, 1), dev(du=1), s, r_xy.at[r + 4])
            push(zp, line_b(zp, u, 0), dev(du=-1), s, r_xy.at[r + 4])
        else:
            push(zp, mc.at[slab_of(zp), v], dev(dv=1), s, r_xy.at[r + 2])
            push(zp, mc.at[slab_of(zp), v], dev(dv=-1), s, r_xy.at[r + 3])

    def xy_forward(slot, zp):
        ul, ur = (u + 3) % NX, (u + 1) % NX
        vl, vr = (v + 3) % NY, (v + 1) % NY
        todo = [
            (B0, line_b(zp, ul, 0), dev(du=1)),
            (B1, line_b(zp, ur, 1), dev(du=-1)),
            (C0, mc.at[slab_of(zp), vl, pl.ds(0, 2)], dev(dv=1)),
            (C0, mc.at[slab_of(zp), vr, pl.ds(2, 2)], dev(dv=-1)),
        ]
        for n, (size, src, target) in enumerate(todo):
            arrive(zp, r_xy.at[5 * slot + n], size)
            push(zp, src, target, s_xy, r_xy.at[5 * slot + 4])

    def at(d):
        return (z + d + NZ) % NZ

    SLOT = {0: 0, -1: 1, 1: 2, -2: 3, 2: 4, -3: 5, 3: 6, 4: 7}

    def z_step(dist, kind):
        if dist == 4:
            z_arrive(0 if kind == "b" else 1, 4, at(4), kind)
            xy_send(7, at(4), kind)
            return
        for g in (0, 1):
            delta = -dist if g == 0 else dist
            z_arrive(g, dist, at(delta), kind)
            if dist < 3:
                z_send(g, dist + 1, at(delta), kind)
            if dist == 2 and kind == "bc"[g]:
                z_send(g, 4, at(delta), kind)
            xy_send(SLOT[delta], at(delta), kind)

    def blk(zp, h, j):
        ref, lane = (ma, 0) if j == 0 else (mb, min(j - 1, 3)) if j <= 3 or j == 7 else (mc, j - 4)
        return ref[zp, 2 * h:2 * h + 2, :, :, 128 * lane:128 * lane + 128].reshape(128, 128)

    def own_rows(i):
        return pfull[:, pl.ds(pl.multiple_of(MXU * i, MXU), MXU)]

    def set_diagonal(i):
        upper = blk(i, 0, 1)
        wn[0:128, 0:128] = blk(i, 0, 0)
        wn[0:128, 128:256] = upper
        wn[128:256, 0:128] = upper.astype(F32).T.astype(BF16)
        wn[128:256, 128:256] = blk(i, 1, 0)

    def compute(zp, whole):
        i = slab_of(zp)

        @pl.when(zp != EMPTY)
        def _():
            if whole:
                set_diagonal(i)
            for d in (1, 2, 3):
                wn[0:128, 256 * d:256 * d + 128] = blk(i, 0, 2 * d)
                wn[0:128, 256 * d + 128:256 * d + 256] = blk(i, 0, 2 * d + 1)
                wn[128:256, 256 * d:256 * d + 128] = blk(i, 1, 2 * d - 1)
                wn[128:256, 256 * d + 128:256 * d + 256] = blk(i, 1, 2 * d)
            own = own_rows(i)
            for d in (1, 2, 3):
                acc[(i + d) % 7] += nn(own, wn[:, 256 * d:256 * d + 256])
            total = nt(own_rows((i + 1) % 7), wn[:, 256:512])
            for d in (2, 3):
                total += nt(own_rows((i + d) % 7), wn[:, 256 * d:256 * d + 256])
            if whole:
                total += nn(own, wn[:, 0:256])
            acc[i] += total

    def diagonals():
        @pl.loop(0, 3)
        def _(n):
            i = slab_of(at(n - 1))

            @pl.when(at(n - 1) != EMPTY)
            def _():
                set_diagonal(i)
                acc[i] += nn(own_rows(i), wn[:, 0:256])

    def forward(dist):
        for delta in ((0,) if dist == 0 else (4,) if dist == 4 else (-dist, dist)):
            xy_forward(SLOT[delta], at(delta))

    def finish(dist):
        for delta in ((0,) if dist == 0 else (4,) if dist == 4 else (-dist, dist)):
            arrive(at(delta), r_xy.at[5 * SLOT[delta] + 4], 2 * (B0 + B1) + C0)
        if dist in (0, 4):
            compute(at(dist), dist > 1)
        else:
            @pl.loop(0, 2)
            def _(n):
                compute(at((2 * n - 1) * dist), dist > 1)

    arrive(z, r_1.at[0], 3 * TILE * 512)
    xy_send(0, z, "b")
    arrive(z, r_1.at[1], 3 * TILE * 384)
    xy_send(0, z, "c")

    A0 = 7 * TILE * 128

    def push_a(src, target, n, m):
        pltpu.make_async_remote_copy(src, src, s_a.at[n], r_a.at[m], device_id=target,
                                     device_id_type=MESH).start()

    @pl.when(z == EMPTY)
    def _():
        drain(r_a.at[0], A0)

    @pl.when(z != EMPTY)
    def _():
        drain(r_a.at[0], 6 * TILE * 128)

    for d in (1, 2, 3):
        push_a(ma.at[:, v, u], dev(du=d), 0, 1)
    z_step(1, "b")
    z_step(1, "c")
    forward(0)
    drain(r_a.at[1], 3 * A0)
    push_a(ma.at[:, v], dev(dv=1), 1, 2)
    push_a(ma.at[:, v], dev(dv=-1), 1, 3)
    z_step(2, "b")
    z_step(2, "c")
    forward(1)
    z_step(3, "b")
    z_step(3, "c")
    z_step(4, "b")
    z_step(4, "c")
    l_pd.wait()
    d_p.wait_recv()
    finish(0)
    forward(2)
    drain(r_a.at[2], 4 * A0)
    push_a(ma.at[:, (v + 3) % NY, pl.ds(0, 2)], dev(dv=1), 1, 4)
    drain(r_a.at[3], 4 * A0)
    push_a(ma.at[:, (v + 1) % NY, pl.ds(2, 2)], dev(dv=-1), 1, 4)
    finish(1)
    forward(3)
    forward(4)
    drain(r_a.at[4], 4 * A0)
    diagonals()
    finish(2)
    finish(3)
    finish(4)

    d_q.wait_recv()

    @pl.loop(0, KP // 4, unroll=True)
    def _(a):
        rows = pl.ds(160 * a, 160)
        scr = jnp.concatenate([acc[b, rows, :].astype(BF16) for b in range(7)], axis=1)
        r = nt(scr, qfull[rows, :])
        for h in range(4):
            slot = lax.broadcasted_iota(jnp.int32, (SLOTS, PC), 0)
            block = r[40 * h:40 * h + 40, 40 * h:40 * h + 40]
            kp[4 * a + h] = jnp.where(slot < cnt[4 * a + h], block, 0.0)

    for p in range(SLOTS):
        mine[:, 40 * p:40 * p + 40] = kp[:, p, :]

    d_o = pltpu.make_async_remote_copy(mine, other, s_d2d.at[2], r_d2d.at[2], device_id=sibling, device_id_type=MESH)
    d_o.start()

    d_p.wait_send()
    d_q.wait_send()
    drain(s_a.at[0], 3 * A0)
    drain(s_a.at[1], 12 * A0)
    drain(s_xy, SLABS * 3 * (B0 + B1 + C0))
    for zp, sem, elements in sends:
        arrive(zp, sem, elements)
    for cond, copy in p0:
        @pl.when(cond)
        def _(copy=copy):
            copy.wait_send()

    d_o.wait_recv()
    point = lax.broadcasted_iota(jnp.int32, (KP, 1), 0)
    first_tile = jnp.zeros((KP, 1), jnp.int32)
    for k in range(KP):
        first_tile = jnp.where(point == k, qs[0, k], first_tile)
    a, b = mine[...], other[...]
    out[0] = jnp.where(first_tile == ga, a, b)
    out[1] = jnp.where(first_tile == ga, b, a)
    d_o.wait_send()


def local(pair_dens, counts, q_index, w_tiles, partner):
    anyspace = pl.BlockSpec(memory_space=pl.ANY)
    vmem = pl.BlockSpec(memory_space=pltpu.VMEM)
    dma = pltpu.SemaphoreType.DMA
    res = pl.pallas_call(
        kernel,
        out_shape=jax.ShapeDtypeStruct((2, KP, SLOTS * PC), F32),
        in_specs=[anyspace] * 5,
        out_specs=vmem,
        scratch_shapes=[
            pltpu.SMEM((KP,), jnp.int32),
            pltpu.SMEM((2, KP), jnp.int32),
            pltpu.VMEM((ROWS, NG), BF16),
            pltpu.VMEM((ROWS, NG), BF16),
            pltpu.VMEM((2 * ROWS, HALF), BF16),
            pltpu.VMEM((ROWS, HALF), BF16),
            pltpu.VMEM((SLABS, NY, NX, TILE, 128), BF16),
            pltpu.VMEM((SLABS, NY, NX, TILE, 512), BF16),
            pltpu.VMEM((SLABS, NY, NX, TILE, 384), BF16),
            pltpu.VMEM((7, ROWS, MXU), F32),
            pltpu.VMEM((2, TILE, WIN * BLK), BF16),
            pltpu.VMEM((OWN_ROWS, 2, HALF), BF16),
            pltpu.VMEM((2, 2, TILE, HALF), BF16),
            pltpu.VMEM((MXU, 4 * MXU), BF16),
            pltpu.VMEM((KP, SLOTS, PC), F32),
            pltpu.VMEM((KP, SLOTS * PC), F32),
            pltpu.VMEM((KP, SLOTS * PC), F32),
            dma((5,)),
            dma((12,)), dma(()),
            dma((3,)), dma((3,)),
            dma(()), dma((2,)),
            dma((2,)), dma((5,)),
            dma((8,)), dma((16,)),
            dma(()), dma((40,)),
        ],
        compiler_params=pltpu.CompilerParams(
            collective_id=0, has_side_effects=True, vmem_limit_bytes=60 * 2**20),
        cost_estimate=pl.CostEstimate(flops=2 * ROWS * NG * NG, bytes_accessed=8 * 2**20, transcendentals=0),
    )(
        pair_dens.reshape(ROWS, HALF),
        partner.reshape(2 * ROWS, HALF),
        jnp.transpose(w_tiles, (2, 0, 1)),
        counts,
        jnp.transpose(q_index),
    )
    return jnp.transpose(res, (1, 0, 2))


def solution(mesh):
    in_specs = (
        P("ka", None, "ga"),
        P("ka"),
        P("ka", None),
        P(None, "ga", "ka"),
        P("ka", None, None, "ga"),
    )
    return jax.shard_map(local, mesh=mesh, in_specs=in_specs, out_specs=P("ka", None, None), check_vma=False)
```
